32 devices in a mesh: aux: 4 (over y, x), pair: 8 (over z, core).
Axes of the slice: x: 2, y: 2, z: 4, core: 2. Of those that a mesh axis runs over, the one named last changes fastest.
Arguments:
- df_tiles: bfloat16 [8, 128, 128, 128], P('pair', 'aux'), as said below
- pno_coeffs: bfloat16 [64, 3, 128, 64], P('pair'), may hold values from -0.5 to 0.5
- domains: int32 [64, 3], P('pair'), may hold values from 0 to 7, all different within a row; in each aligned block of 8 rows (0 to 7, 8 to 15, ...) at most 3 rows name the same one
- amplitudes: float32 [64, 64, 64], P('pair'), may hold values from -0.6 to 0.6
- exchange_ints: float32 [64, 64, 64], P('pair'), may hold values from -3 to 3
- pno_energy: float32 [64, 64], P('pair'), may hold values from 0.2 to 4
- pair_shift: float32 [64], P('pair'), may hold values from 0.3 to 1.5
- pno_count: int32 [64], P('pair'), may hold values from 16 to 64
Outputs:
- updated: float32 [64, 64, 64], P('pair')
The draws below stay inside these ranges and needn't reach their ends.
Inputs may be any that keep to these rules, and one draw needn't show every extreme that they name: `domains`: among the pairs of one device no block is named by more than 3 pairs, and some block is named by exactly 3 of them. `df_tiles`: each tile is symmetric in its two PAO indices.
All inputs are finite; a program needn't handle non-finite values.
Results may differ from the reference program's by a relative error of at most 0.018.
Values may be sent and summed in bfloat16 or wider, within the bound.
A program may use at most 256 MiB of HBM per device.

```python
import math
import jax
import jax.numpy as jnp
import numpy as np
from jax import lax

NPNO = 64
PB = 128
DB = 3
QA = 128
P_DEV = 8
BLOCKS = 8
PAIRS = 64
CAP = 3


def draw_df_tiles(key, part):
    key = jax.random.fold_in(key, 11)
    factor = (8.0 * DB * math.sqrt(QA)) ** (-0.5)
    shape = (BLOCKS, QA, PB, PB)
    raw = jax.random.normal(key, shape, jnp.float32)
    sym = (raw + jnp.swapaxes(raw, -1, -2)) * 0.70710678
    return (jnp.clip(sym, -4.0, 4.0) * factor).astype(jnp.bfloat16)


def with_ends(array, key, least, top_value):
    extent = array.shape
    spot = [jax.random.randint(jax.random.fold_in(key, axis), (), 0, extent[axis]) for axis in range(len(extent))]
    array = array.at[tuple(spot)].set(least)
    longest = extent.index(max(extent))
    spot[longest] = (spot[longest] + 1) % extent[longest]
    return array.at[tuple(spot)].set(top_value)


def levels(stream_key, shape, shards, low, top_value):
    factor_of = 1.0
    for position, parts in shards:
        steps = jax.random.uniform(jax.random.fold_in(jax.random.fold_in(stream_key, 6), position), (parts,), jnp.float32, low / len(shards), top_value / len(shards))
        factor_of = factor_of * jnp.repeat(jnp.exp(steps), shape[position] // parts).reshape((-1,) + (1,) * (len(shape) - 1 - position))
    return factor_of


def assign_block(rng, own, number, rows, number_of, top, reach, skew):
    ranking = jax.random.permutation(rng, number_of)
    packed, ordinary = load_shares(number_of, rows * top, reach, skew, True), load_shares(number_of, rows * top, reach, skew, False)
    places = jnp.arange(number_of)

    def named(tallies, turn):
        used = int((tallies > 0).sum())
        fixed = max(1, used // 4)
        moved = fixed + (places - fixed + turn * (used - fixed)) % max(1, number_of - fixed)
        return jnp.zeros((number_of,), jnp.int32).at[ranking[jnp.where(places < fixed, places, moved)]].set(jnp.asarray(tallies, jnp.int32))

    tallies = jnp.where(number % 4 == 0, named(packed, number // 4), named(ordinary, number - number // 4 - 1))
    mixed = jax.random.permutation(jax.random.fold_in(own, 3), number_of)
    source_of, taker = mixed[0:number_of // 2 * 2:2], mixed[1:number_of // 2 * 2:2]
    margin = jnp.minimum(tallies[source_of] - 1, reach - tallies[taker]) // 2
    margin = jnp.where((source_of == ranking[0]) | (taker == ranking[0]) | (tallies[taker] == 0), 0, jnp.maximum(margin, 0))
    moved = jax.random.randint(jax.random.fold_in(own, 4), (number_of // 2,), 0, 1 << 20) % (margin + 1)
    tallies = tallies.at[source_of].add(-moved).at[taker].add(moved)
    items = jnp.searchsorted(jnp.cumsum(tallies), jnp.arange(rows * top), side="right").astype(jnp.int32)
    listing = items.reshape(top, rows).T
    listing = listing[jax.random.permutation(jax.random.fold_in(own, 1), rows)]
    turn = jax.random.randint(jax.random.fold_in(own, 2), (rows, 1), 0, top)
    return jnp.take_along_axis(listing, (jnp.arange(top)[None, :] + turn) % top, axis=1)


def load_shares(count, total, limit, skew, full):
    weights = [(1 << 20) // math.isqrt(rank ** skew) + 1 for rank in range(1, count + 1)]
    largest = limit if full else min(limit, max(-(-total // count), total * weights[0] // sum(weights)))
    least = 1 if total - largest >= count - 1 else 0
    holding, spare = [largest] + [least] * (count - 1), total - largest - least * (count - 1)
    while spare > 0:
        movable = [i for i in range(1, count) if holding[i] < largest] or [i for i in range(1, count) if holding[i] < limit]
        whole, budget = sum([weights[i] for i in movable]), spare
        for i in movable:
            extra = min(limit - holding[i], max(1, budget * weights[i] // whole), spare)
            holding[i] = holding[i] + extra
            spare = spare - extra
    return np.array(holding)


def noise(own_key, dims, spread, bound, cuts=(), kind=jnp.bfloat16):
    values = jax.random.normal(own_key, dims, jnp.float32) * spread
    if len(cuts) > 0:
        values = levels(own_key, dims, cuts, -0.22, 0.18) * values
    return jnp.clip(values, min=-bound, max=bound).astype(kind)


def setup_inputs(seed: int = 0) -> dict:
    splits = jax.random.split(jax.random.key(seed), 9)
    df_tiles = draw_df_tiles(jax.random.fold_in(splits[8], 71), 0)
    pno_coeffs = noise(splits[1], (PAIRS, DB, PB, NPNO), PB ** -0.5, 0.5, ((0, 8),))
    domains_keys = jax.random.split(jax.random.fold_in(splits[2], 1), PAIRS // P_DEV)
    domains_turns = jax.random.permutation(jax.random.fold_in(splits[2], 3), PAIRS // P_DEV)
    domains = jax.vmap(lambda own, number: assign_block(jax.random.fold_in(splits[2], 2), own, number, P_DEV, BLOCKS, DB, CAP, 2))(domains_keys, domains_turns).reshape((PAIRS, DB))
    amplitudes = noise(splits[3], (PAIRS, NPNO, NPNO), 0.1, 0.6, ((0, 8),), jnp.float32)
    exchange_ints = noise(splits[4], (PAIRS, NPNO, NPNO), 0.5, 3.0, ((0, 8),), jnp.float32)
    pno_energy = jnp.clip(jnp.exp(math.log(4.0) - 2.9957323 * jax.random.uniform(splits[5], (PAIRS, NPNO), jnp.float32) ** levels(splits[5], (PAIRS, NPNO), ((0, 8),), -0.2, 0.2)), 0.2, 4.0)
    pair_shift = jnp.clip(jnp.exp(math.log(1.5) - 1.60943787 * jax.random.uniform(splits[6], (PAIRS,), jnp.float32) ** levels(splits[6], (PAIRS,), ((0, 8),), -0.2, 0.2)), 0.3, 1.5)
    pno_count = with_ends(jax.random.randint(splits[7], (PAIRS,), NPNO // 4, NPNO + 1), jax.random.fold_in(splits[7], 1), NPNO // 4, NPNO).astype(jnp.int32)
    return {"df_tiles": df_tiles, "pno_coeffs": pno_coeffs, "domains": domains, "amplitudes": amplitudes, "exchange_ints": exchange_ints, "pno_energy": pno_energy, "pair_shift": pair_shift, "pno_count": pno_count}


def reference(df_tiles, pno_coeffs, domains, amplitudes, exchange_ints, pno_energy, pair_shift, pno_count):
    columns = jnp.arange(NPNO, dtype=jnp.int32)

    def one_pair(items):
        domain, coeffs, trial_amp, exch, energy, shift, count = items
        live = columns < count
        masked = jnp.where(live[None, None, :], coeffs, jnp.zeros_like(coeffs)).astype(jnp.bfloat16)
        total = jnp.zeros((QA, NPNO, NPNO), jnp.float32)
        for block in range(DB):
            block_tile = lax.dynamic_index_in_dim(df_tiles, domain[block].astype(jnp.int32), 0, keepdims=False)
            half = jnp.einsum('qmn,np->qmp', block_tile.astype(jnp.float32), masked[block].astype(jnp.float32)).astype(jnp.bfloat16)
            piece = jnp.einsum('mp,qmr->qpr', masked[block].astype(jnp.float32), half.astype(jnp.float32)).astype(jnp.bfloat16)
            total = total + piece.astype(jnp.float32)
        pair_ints = total.astype(jnp.bfloat16)
        both = live[:, None] & live[None, :]
        trial = jnp.where(both, trial_amp, jnp.zeros_like(trial_amp)).astype(jnp.bfloat16)
        inter = jnp.einsum('qac,cd->qad', pair_ints.astype(jnp.float32), trial.astype(jnp.float32)).astype(jnp.bfloat16)
        ladder = jnp.einsum('qad,qbd->ab', inter.astype(jnp.float32), pair_ints.astype(jnp.float32))
        denom = energy[:, None] + energy[None, :] + shift
        fresh = trial_amp - (exch + ladder) / denom
        return jnp.where(both, fresh, jnp.zeros_like(fresh))

    return lax.map(one_pair, (domains, pno_coeffs, amplitudes, exchange_ints, pno_energy, pair_shift, pno_count))
```

```python
import functools
import math

import jax
import jax.numpy as jnp
from jax import lax
from jax.experimental import pallas as pl
from jax.experimental.pallas import tpu as pltpu
from jax.sharding import PartitionSpec as P


def apply_update(ladder, trial_amp, exch, energy_rows, energy_cols, shift, both):
    denom = energy_rows[:, :, None] + energy_cols[:, None, :] + shift[:, None, None]
    fresh = trial_amp - (exch + ladder) / denom
    return jnp.where(both, fresh, jnp.zeros_like(fresh))


def per_device(
    df_tiles, pno_coeffs, domains, amplitudes, exchange_ints, pno_energy, pair_shift, pno_count
):
    peers = lax.axis_size("pair")
    pair_count, domain_blocks, pao_width, pno_width = pno_coeffs.shape
    aux_local = df_tiles.shape[1]
    capacity = (pair_count * domain_blocks + peers - 1) // peers
    slot_count = peers * capacity
    request_count = pair_count * domain_blocks
    columns = jnp.arange(pno_width, dtype=jnp.int32)
    live = columns[None, :] < pno_count[:, None]
    masked = jnp.where(live[:, None, None, :], pno_coeffs, jnp.zeros_like(pno_coeffs))
    targets = domains.reshape(request_count)
    hits = (targets[:, None] == jnp.arange(peers, dtype=jnp.int32)[None, :]).astype(jnp.int32)
    before = jnp.cumsum(hits, axis=0) - hits
    ranks = jnp.sum(before * hits, axis=1)
    slots = targets * capacity + ranks
    select = (slots[:, None] == jnp.arange(slot_count, dtype=jnp.int32)[None, :]).astype(
        jnp.bfloat16
    )
    flat_coeffs = masked.reshape(request_count, pao_width * pno_width)
    outgoing = jnp.einsum(
        "rs,rk->sk", select, flat_coeffs, preferred_element_type=jnp.float32
    ).astype(jnp.bfloat16)
    outgoing = outgoing.reshape(peers, capacity, pao_width, pno_width)
    own_tile = df_tiles[0]
    arrived = lax.all_to_all(outgoing, "pair", split_axis=0, concat_axis=0, tiled=True)
    sources = arrived.shape[0]
    depth = arrived.shape[1]
    total = sources * depth
    group_size = math.gcd(total, 8)
    grouped = arrived.reshape(total // group_size, group_size, pao_width, pno_width)

    def project_group(group):
        half = jnp.einsum(
            "qmn,snp->sqmp", own_tile, group, preferred_element_type=jnp.float32
        ).astype(jnp.bfloat16)
        return jnp.einsum("smp,sqmr->sqpr", group, half, preferred_element_type=jnp.float32).astype(
            jnp.bfloat16
        )

    pieces = lax.map(project_group, grouped).reshape(
        sources, depth, aux_local, pno_width, pno_width
    )
    packed = pieces.reshape(sources, depth, aux_local * pno_width * pno_width)
    returned = lax.all_to_all(packed, "pair", split_axis=0, concat_axis=0, tiled=True)
    returned = returned.reshape(slot_count, returned.shape[2])
    owner_pair = jnp.arange(request_count, dtype=jnp.int32) // domain_blocks
    owner_sel = (owner_pair[:, None] == jnp.arange(pair_count, dtype=jnp.int32)[None, :]).astype(
        jnp.bfloat16
    )
    pair_sel = jnp.einsum(
        "rp,rs->ps", owner_sel, select, preferred_element_type=jnp.float32
    ).astype(jnp.bfloat16)
    sums = jnp.dot(pair_sel, returned, preferred_element_type=jnp.float32)
    full = sums.reshape(pair_count, aux_local, pno_width, pno_width)
    pair_ints = full.astype(jnp.bfloat16)
    both = live[:, :, None] & live[:, None, :]
    trial = jnp.where(both, amplitudes, jnp.zeros_like(amplitudes)).astype(jnp.bfloat16)
    inter = jnp.einsum(
        "pqac,pcd->pqad", pair_ints, trial, preferred_element_type=jnp.float32
    ).astype(jnp.bfloat16)
    partial_ladder = jnp.einsum(
        "pqad,pqbd->pab", inter, pair_ints, preferred_element_type=jnp.float32
    )
    ladder = lax.psum(partial_ladder.astype(jnp.bfloat16), "aux").astype(jnp.float32)
    return apply_update(ladder, amplitudes, exchange_ints, pno_energy, pno_energy, pair_shift, both)


MESH = pl.DeviceIdType.MESH


def ladder_kernel(packed_ref, coeff_ref, slot_ref, trial_ref, out_ref, tiles, halves, pieces,
                  shares, send_sem, recv_sem, pass_send, pass_recv, twin_sem, aux_send, aux_recv,
                  *, depth):
    aux, pair = lax.axis_index("aux"), lax.axis_index("pair")
    peers, groups = tiles.shape[0], shares.shape[0]
    quarter = halves.shape[1] // (tiles.shape[3] // 2)
    width = tiles.shape[3] // 2
    pairs = trial_ref.shape[0]
    domain = slot_ref.shape[0] // pairs
    chip, core = pair // 2, pair % 2
    twin = chip * 2 + 1 - core
    chips = (chip + 1 - 2 * (chip % 2), 3 - chip, (chip + 2) % 4)

    barrier = pltpu.get_barrier_semaphore()
    for step in range(1, peers):
        pl.semaphore_signal(barrier, inc=1, device_id={"pair": lax.rem(pair + step, peers)}, device_id_type=MESH)
    for step in range(1, groups):
        pl.semaphore_signal(barrier, inc=1, device_id={"aux": lax.rem(aux + step, groups)}, device_id_type=MESH)
    pl.semaphore_wait(barrier, peers + groups - 2)

    sends = []
    for hop in range(3):
        for side in range(2):
            slot = hop * 2 + side
            copy = pltpu.make_async_remote_copy(
                src_ref=packed_ref.at[side],
                dst_ref=tiles.at[pair, side],
                send_sem=send_sem.at[slot],
                recv_sem=recv_sem.at[hop * 2 + core],
                device_id={"pair": chips[hop] * 2 + side},
                device_id_type=MESH,
            )
            copy.start()
            sends.append(copy)
    whole = pltpu.make_async_remote_copy(
        src_ref=packed_ref,
        dst_ref=tiles.at[pair],
        send_sem=twin_sem.at[0],
        recv_sem=twin_sem.at[1],
        device_id={"pair": twin},
        device_id_type=MESH,
    )
    whole.start()

    row = lax.broadcasted_iota(jnp.int32, (width, 2 * width), 0)
    lane = lax.broadcasted_iota(jnp.int32, (width, 2 * width), 1)
    upper = lane >= row
    corner = lane == row + width
    unroll = 4

    def project(source, block, part):
        coeffs = coeff_ref[block]

        def some(group, carry):
            for inner in range(unroll):
                aux_fn = group * unroll + inner
                first = pl.multiple_of(aux_fn * width, width)
                folded = source(pl.ds(first, width)).astype(jnp.float32)
                edge = source(pl.ds(pl.multiple_of(quarter * width + group * 16, 16), 16))
                edge = edge[inner:inner + 1].astype(jnp.float32)
                top = jnp.where(upper, folded, 0.0)
                low = pltpu.roll(jnp.where(upper, 0.0, folded), width, 1)
                low = jnp.where(corner, edge, low)
                tri = jnp.concatenate([top, low], axis=0).astype(jnp.bfloat16)
                half = jnp.dot(coeffs, tri, preferred_element_type=jnp.float32)
                half += lax.dot_general(coeffs, tri, (((1,), (1,)), ((), ())), preferred_element_type=jnp.float32)
                half = half.astype(jnp.bfloat16)
                for rank in range(depth):
                    halves[rank, pl.ds(first, width), :] = half[rank * width:(rank + 1) * width]
            return carry

        lax.fori_loop(0, quarter // unroll, some, 0)
        span = quarter * width
        for rank in range(depth):
            piece = lax.dot_general(
                coeffs[rank * width:(rank + 1) * width], halves[rank],
                (((1,), (1,)), ((), ())), preferred_element_type=jnp.float32,
            )
            pieces[block * depth + rank, :, pl.ds(pl.multiple_of(part * span, span), span)] = piece.astype(jnp.bfloat16)

    def own(part, carry):
        project(lambda rows: packed_ref[part, rows, :], pair, part)
        return carry

    def arrived(block, part):
        project(lambda rows: tiles[block, part, rows, :], block, part)

    lax.fori_loop(0, 2, own, 0)
    whole.wait_recv()

    def from_twin(part, carry):
        arrived(twin, part)
        return carry

    lax.fori_loop(0, 2, from_twin, 0)

    passes = []
    for hop in range(3):
        handed = []
        for side in range(2):
            slot = hop * 2 + side
            block = chips[hop] * 2 + side
            pltpu.make_async_remote_copy(
                src_ref=packed_ref.at[side], dst_ref=tiles.at[block, core],
                send_sem=send_sem.at[slot], recv_sem=recv_sem.at[slot],
                device_id={"pair": block}, device_id_type=MESH,
            ).wait_recv()
            copy = pltpu.make_async_remote_copy(
                src_ref=tiles.at[block, core],
                dst_ref=tiles.at[block, core],
                send_sem=pass_send.at[slot],
                recv_sem=pass_recv.at[slot],
                device_id={"pair": twin},
                device_id_type=MESH,
            )
            copy.start()
            handed.append(copy)
        passes += handed

        def direct(side, carry, hop=hop):
            arrived(chips[hop] * 2 + side, core)
            return carry

        lax.fori_loop(0, 2, direct, 0)
        for side in range(2):
            slot = hop * 2 + side
            block = chips[hop] * 2 + side
            pltpu.make_async_remote_copy(
                src_ref=tiles.at[block, core], dst_ref=tiles.at[block, 1 - core],
                send_sem=pass_send.at[slot], recv_sem=pass_recv.at[slot],
                device_id={"pair": twin}, device_id_type=MESH,
            ).wait_recv()

        def passed(side, carry, hop=hop):
            arrived(chips[hop] * 2 + side, 1 - core)
            return carry

        lax.fori_loop(0, 2, passed, 0)

    def ladder_of(index):
        total = pieces[slot_ref[index * domain]].astype(jnp.float32)
        for step in range(1, domain):
            total += pieces[slot_ref[index * domain + step]].astype(jnp.float32)
        ints = total.astype(jnp.bfloat16)
        trial = trial_ref[index]
        span = trial.shape[0]
        inter = jnp.concatenate(
            [
                jnp.dot(ints[:, at:at + span], trial, preferred_element_type=jnp.float32).astype(jnp.bfloat16)
                for at in range(0, ints.shape[1], span)
            ],
            axis=1,
        )
        return lax.dot_general(inter, ints, (((1,), (1,)), ((), ())), preferred_element_type=jnp.float32)

    def ladders(index, carry):
        both = jnp.concatenate([ladder_of(index), ladder_of(index + pairs // 2)], axis=1)
        shares[aux, pl.ds(pl.multiple_of(index * width, width), width), :] = both.astype(jnp.bfloat16)
        return carry

    lax.fori_loop(0, pairs // 2, ladders, 0)
    exchange = []
    for step in range(1, groups):
        copy = pltpu.make_async_remote_copy(
            src_ref=shares.at[aux],
            dst_ref=shares.at[aux],
            send_sem=aux_send.at[step - 1],
            recv_sem=aux_recv.at[step - 1],
            device_id={"aux": lax.rem(aux + step, groups)},
            device_id_type=MESH,
        )
        copy.start()
        exchange.append(copy)
    for copy in sends + passes + [whole]:
        copy.wait_send()
    for step in range(1, groups):
        sender = lax.rem(aux + groups - step, groups)
        pltpu.make_async_remote_copy(
            src_ref=shares.at[aux], dst_ref=shares.at[sender],
            send_sem=aux_send.at[step - 1], recv_sem=aux_recv.at[step - 1],
            device_id={"aux": sender}, device_id_type=MESH,
        ).wait_recv()
        exchange[step - 1].wait_send()
    result = shares[0].astype(jnp.float32)
    for step in range(1, groups):
        result += shares[step].astype(jnp.float32)
    out_ref[...] = result


def fold_tiles(own_tile):
    count, rows, _ = own_tile.shape
    width = rows // 2
    row = lax.broadcasted_iota(jnp.int32, (width, rows), 0)
    lane = lax.broadcasted_iota(jnp.int32, (width, rows), 1)
    top, bottom = own_tile[:, :width], own_tile[:, width:]
    folded = jnp.where(lane >= row, top, jnp.roll(bottom, width, axis=2))
    folded = jnp.where(lane == row, folded * jnp.bfloat16(0.5), folded)
    edge = jnp.sum(jnp.where(lane == row + width, bottom.astype(jnp.float32) * 0.5, 0.0), axis=1)
    edge = edge.astype(jnp.bfloat16).reshape(count // 4, 4, rows)
    edge = jnp.pad(edge, ((0, 0), (0, 12), (0, 0))).reshape(2, -1, rows)
    return jnp.concatenate([folded.reshape(2, -1, rows), edge], axis=1)


def per_device_gathered(
    df_tiles, pno_coeffs, domains, amplitudes, exchange_ints, pno_energy, pair_shift, pno_count
):
    peers, groups = lax.axis_size("pair"), lax.axis_size("aux")
    pair_count, domain_blocks, pao_width, width = pno_coeffs.shape
    request_count = pair_count * domain_blocks
    depth = request_count // peers
    columns = jnp.arange(width, dtype=jnp.int32)
    live = columns[None, :] < pno_count[:, None]
    masked = jnp.where(live[:, None, None, :], pno_coeffs, jnp.zeros_like(pno_coeffs))
    targets = domains.reshape(request_count)
    order = jnp.arange(request_count, dtype=jnp.int32)
    earlier = (targets[:, None] == targets[None, :]) & (order[None, :] < order[:, None])
    slots = targets * depth + jnp.sum(earlier.astype(jnp.int32), axis=1)
    select = (slots[:, None] == order[None, :]).astype(jnp.bfloat16)
    coeffs = jnp.einsum(
        "rs,rnb->sbn", select, masked.reshape(request_count, pao_width, width),
        preferred_element_type=jnp.float32,
    ).astype(jnp.bfloat16)
    coeffs = coeffs.reshape(peers, depth * width, pao_width)
    both = live[:, :, None] & live[:, None, :]
    trial = jnp.where(both, amplitudes, jnp.zeros_like(amplitudes)).astype(jnp.bfloat16)
    twice = jnp.arange(2 * width, dtype=jnp.int32) // width
    trial = jnp.where(twice[:, None] == twice[None, :], jnp.tile(trial, (1, 2, 2)), jnp.bfloat16(0))
    packed = fold_tiles(df_tiles[0])
    rows = packed.shape[1]
    quarter = df_tiles.shape[1] // 2
    vmem = pl.BlockSpec(memory_space=pltpu.VMEM)
    dma = pltpu.SemaphoreType.DMA
    ladder = pl.pallas_call(
        functools.partial(ladder_kernel, depth=depth),
        out_shape=jax.ShapeDtypeStruct((pair_count // 2 * width, 2 * width), jnp.float32),
        in_specs=[vmem, vmem, pl.BlockSpec(memory_space=pltpu.SMEM), vmem],
        out_specs=vmem,
        scratch_shapes=[
            pltpu.VMEM((peers, 2, rows, pao_width), jnp.bfloat16),
            pltpu.VMEM((depth, quarter * width, pao_width), jnp.bfloat16),
            pltpu.VMEM((request_count, width, 2 * quarter * width), jnp.bfloat16),
            pltpu.VMEM((groups, pair_count // 2 * width, 2 * width), jnp.bfloat16),
            dma((6,)), dma((6,)), dma((6,)), dma((6,)), dma((2,)),
            dma((groups - 1,)), dma((groups - 1,)),
        ],
        compiler_params=pltpu.CompilerParams(
            collective_id=0, has_side_effects=True, vmem_limit_bytes=48 * 1024 * 1024
        ),
        cost_estimate=pl.CostEstimate(flops=4000000000, bytes_accessed=4000000, transcendentals=0),
    )(packed, coeffs, slots, trial)
    ladder = ladder.reshape(pair_count // 2, width, 2, width).transpose(2, 0, 1, 3)
    ladder = ladder.reshape(pair_count, width, width)
    return apply_update(ladder, amplitudes, exchange_ints, pno_energy, pno_energy, pair_shift, both)


def solution(mesh):
    placed = (
        P("pair", "aux", None, None),
        P("pair", None, None, None),
        P("pair", None),
        P("pair", None, None),
        P("pair", None, None),
        P("pair", None),
        P("pair"),
        P("pair"),
    )
    body = per_device_gathered if mesh.shape["pair"] == 8 else per_device
    return jax.shard_map(
        body, mesh=mesh, in_specs=placed, out_specs=P("pair", None, None), check_vma=False
    )
```

```python
import functools
import math

import jax
import jax.numpy as jnp
from jax import lax
from jax.experimental import pallas as pl
from jax.experimental.pallas import tpu as pltpu
from jax.sharding import PartitionSpec as P


def apply_update(ladder, trial_amp, exch, energy_rows, energy_cols, shift, both):
    denom = energy_rows[:, :, None] + energy_cols[:, None, :] + shift[:, None, None]
    fresh = trial_amp - (exch + ladder) / denom
    return jnp.where(both, fresh, jnp.zeros_like(fresh))


def per_device(
    df_tiles, pno_coeffs, domains, amplitudes, exchange_ints, pno_energy, pair_shift, pno_count
):
    peers = lax.axis_size("pair")
    pair_count, domain_blocks, pao_width, pno_width = pno_coeffs.shape
    aux_local = df_tiles.shape[1]
    capacity = (pair_count * domain_blocks + peers - 1) // peers
    slot_count = peers * capacity
    request_count = pair_count * domain_blocks
    columns = jnp.arange(pno_width, dtype=jnp.int32)
    live = columns[None, :] < pno_count[:, None]
    masked = jnp.where(live[:, None, None, :], pno_coeffs, jnp.zeros_like(pno_coeffs))
    targets = domains.reshape(request_count)
    hits = (targets[:, None] == jnp.arange(peers, dtype=jnp.int32)[None, :]).astype(jnp.int32)
    before = jnp.cumsum(hits, axis=0) - hits
    ranks = jnp.sum(before * hits, axis=1)
    slots = targets * capacity + ranks
    select = (slots[:, None] == jnp.arange(slot_count, dtype=jnp.int32)[None, :]).astype(
        jnp.bfloat16
    )
    flat_coeffs = masked.reshape(request_count, pao_width * pno_width)
    outgoing = jnp.einsum(
        "rs,rk->sk", select, flat_coeffs, preferred_element_type=jnp.float32
    ).astype(jnp.bfloat16)
    outgoing = outgoing.reshape(peers, capacity, pao_width, pno_width)
    own_tile = df_tiles[0]
    arrived = lax.all_to_all(outgoing, "pair", split_axis=0, concat_axis=0, tiled=True)
    sources = arrived.shape[0]
    depth = arrived.shape[1]
    total = sources * depth
    group_size = math.gcd(total, 8)
    grouped = arrived.reshape(total // group_size, group_size, pao_width, pno_width)

    def project_group(group):
        half = jnp.einsum(
            "qmn,snp->sqmp", own_tile, group, preferred_element_type=jnp.float32
        ).astype(jnp.bfloat16)
        return jnp.einsum("smp,sqmr->sqpr", group, half, preferred_element_type=jnp.float32).astype(
            jnp.bfloat16
        )

    pieces = lax.map(project_group, grouped).reshape(
        sources, depth, aux_local, pno_width, pno_width
    )
    packed = pieces.reshape(sources, depth, aux_local * pno_width * pno_width)
    returned = lax.all_to_all(packed, "pair", split_axis=0, concat_axis=0, tiled=True)
    returned = returned.reshape(slot_count, returned.shape[2])
    owner_pair = jnp.arange(request_count, dtype=jnp.int32) // domain_blocks
    owner_sel = (owner_pair[:, None] == jnp.arange(pair_count, dtype=jnp.int32)[None, :]).astype(
        jnp.bfloat16
    )
    pair_sel = jnp.einsum(
        "rp,rs->ps", owner_sel, select, preferred_element_type=jnp.float32
    ).astype(jnp.bfloat16)
    sums = jnp.dot(pair_sel, returned, preferred_element_type=jnp.float32)
    full = sums.reshape(pair_count, aux_local, pno_width, pno_width)
    pair_ints = full.astype(jnp.bfloat16)
    both = live[:, :, None] & live[:, None, :]
    trial = jnp.where(both, amplitudes, jnp.zeros_like(amplitudes)).astype(jnp.bfloat16)
    inter = jnp.einsum(
        "pqac,pcd->pqad", pair_ints, trial, preferred_element_type=jnp.float32
    ).astype(jnp.bfloat16)
    partial_ladder = jnp.einsum(
        "pqad,pqbd->pab", inter, pair_ints, preferred_element_type=jnp.float32
    )
    ladder = lax.psum(partial_ladder.astype(jnp.bfloat16), "aux").astype(jnp.float32)
    return apply_update(ladder, amplitudes, exchange_ints, pno_energy, pno_energy, pair_shift, both)


MESH = pl.DeviceIdType.MESH


def ladder_kernel(packed_ref, coeff_ref, slot_ref, trial_ref, out_ref, tiles, halves, pieces,
                  shares, first_send, link_send, link_recv, pass_send, pass_recv, twin_sem, aux_send,
                  aux_recv,
                  *, depth):
    aux, pair = lax.axis_index("aux"), lax.axis_index("pair")
    peers, groups = tiles.shape[0], shares.shape[0]
    quarter = halves.shape[1] // (tiles.shape[3] // 2)
    width = tiles.shape[3] // 2
    pairs = trial_ref.shape[0]
    domain = slot_ref.shape[0] // pairs
    chip, core = pair // 2, pair % 2
    twin = chip * 2 + 1 - core
    last = peers // 2 - 1

    barrier = pltpu.get_barrier_semaphore()
    for step in range(1, peers):
        pl.semaphore_signal(barrier, inc=1, device_id={"pair": lax.rem(pair + step, peers)}, device_id_type=MESH)
    for step in range(1, groups):
        pl.semaphore_signal(barrier, inc=1, device_id={"aux": lax.rem(aux + step, groups)}, device_id_type=MESH)
    pl.semaphore_wait(barrier, peers + groups - 2)

    def remote(source, target, send, recv, where):
        return pltpu.make_async_remote_copy(
            src_ref=source, dst_ref=target, send_sem=send, recv_sem=recv,
            device_id={"pair": where}, device_id_type=MESH,
        )

    def onward(way):
        return chip + 1 if way == 0 else chip - 1

    def can_send(way):
        return chip < last if way == 0 else chip > 0

    def has_source(far, way):
        return chip >= far if way == 0 else chip + far <= last

    def block_of(far, way, side):
        return (chip - far if way == 0 else chip + far) * 2 + side

    def number(far, way, side):
        return ((far - 1) * 2 + way) * 2 + side

    def first(way, side):
        return remote(packed_ref.at[side], tiles.at[pair, side], first_send.at[way * 2 + side],
                      link_recv.at[number(1, way, core)], onward(way) * 2 + side)

    def link(far, way, side):
        block = block_of(far, way, side)
        return remote(tiles.at[block, core], tiles.at[block, core], link_send.at[number(far, way, side)],
                      link_recv.at[number(far + 1, way, side)], onward(way) * 2 + core)

    def incoming(far, way, side):
        block = block_of(far, way, side)
        return remote(packed_ref.at[0], tiles.at[block, core], link_send.at[number(far, way, side)],
                      link_recv.at[number(far, way, side)], twin)

    def handed(far, way, side):
        block = block_of(far, way, side)
        return remote(tiles.at[block, core], tiles.at[block, core], pass_send.at[number(far, way, side)],
                      pass_recv.at[number(far, way, side)], twin)

    def handed_here(far, way, side):
        block = block_of(far, way, side)
        return remote(packed_ref.at[0], tiles.at[block, 1 - core], pass_send.at[number(far, way, side)],
                      pass_recv.at[number(far, way, side)], twin)

    for way in range(2):
        @pl.when(can_send(way))
        def _(way=way):
            for side in range(2):
                first(way, side).start()

    whole = pltpu.make_async_remote_copy(
        src_ref=packed_ref,
        dst_ref=tiles.at[pair],
        send_sem=twin_sem.at[0],
        recv_sem=twin_sem.at[1],
        device_id={"pair": twin},
        device_id_type=MESH,
    )
    whole.start()

    row = lax.broadcasted_iota(jnp.int32, (width, 2 * width), 0)
    lane = lax.broadcasted_iota(jnp.int32, (width, 2 * width), 1)
    upper = lane >= row
    corner = lane == row + width
    unroll = 4

    def project(source, block, part):
        coeffs = coeff_ref[block]

        def some(group, carry):
            for inner in range(unroll):
                aux_fn = group * unroll + inner
                first = pl.multiple_of(aux_fn * width, width)
                folded = source(pl.ds(first, width)).astype(jnp.float32)
                edge = source(pl.ds(pl.multiple_of(quarter * width + group * 16, 16), 16))
                edge = edge[inner:inner + 1].astype(jnp.float32)
                top = jnp.where(upper, folded, 0.0)
                low = pltpu.roll(jnp.where(upper, 0.0, folded), width, 1)
                low = jnp.where(corner, edge, low)
                tri = jnp.concatenate([top, low], axis=0).astype(jnp.bfloat16)
                half = jnp.dot(coeffs, tri, preferred_element_type=jnp.float32)
                half += lax.dot_general(coeffs, tri, (((1,), (1,)), ((), ())), preferred_element_type=jnp.float32)
                half = half.astype(jnp.bfloat16)
                for rank in range(depth):
                    halves[rank, pl.ds(first, width), :] = half[rank * width:(rank + 1) * width]
            return carry

        lax.fori_loop(0, quarter // unroll, some, 0)
        span = quarter * width
        for rank in range(depth):
            piece = lax.dot_general(
                coeffs[rank * width:(rank + 1) * width], halves[rank],
                (((1,), (1,)), ((), ())), preferred_element_type=jnp.float32,
            )
            pieces[block * depth + rank, :, pl.ds(pl.multiple_of(part * span, span), span)] = piece.astype(jnp.bfloat16)

    def own(part, carry):
        project(lambda rows: packed_ref[part, rows, :], pair, part)
        return carry

    def arrived(block, part):
        project(lambda rows: tiles[block, part, rows, :], block, part)

    lax.fori_loop(0, 2, own, 0)
    whole.wait_recv()

    def from_twin(part, carry):
        arrived(twin, part)
        return carry

    lax.fori_loop(0, 2, from_twin, 0)

    for far in range(1, last + 1):
        for way in range(2):
            @pl.when(has_source(far, way))
            def _(far=far, way=way):
                for side in range(2):
                    incoming(far, way, side).wait_recv()
                    if far < last:
                        @pl.when(can_send(way))
                        def _(side=side):
                            link(far, way, side).start()
                    handed(far, way, side).start()

        for way in range(2):
            @pl.when(has_source(far, way))
            def _(far=far, way=way):
                def direct(side, carry):
                    arrived(block_of(far, way, side), core)
                    return carry

                lax.fori_loop(0, 2, direct, 0)

        for way in range(2):
            @pl.when(has_source(far, way))
            def _(far=far, way=way):
                for side in range(2):
                    handed_here(far, way, side).wait_recv()

                def passed(side, carry):
                    arrived(block_of(far, way, side), 1 - core)
                    return carry

                lax.fori_loop(0, 2, passed, 0)

    def ladder_of(index):
        total = pieces[slot_ref[index * domain]].astype(jnp.float32)
        for step in range(1, domain):
            total += pieces[slot_ref[index * domain + step]].astype(jnp.float32)
        ints = total.astype(jnp.bfloat16)
        trial = trial_ref[index]
        span = trial.shape[0]
        inter = jnp.concatenate(
            [
                jnp.dot(ints[:, at:at + span], trial, preferred_element_type=jnp.float32).astype(jnp.bfloat16)
                for at in range(0, ints.shape[1], span)
            ],
            axis=1,
        )
        return lax.dot_general(inter, ints, (((1,), (1,)), ((), ())), preferred_element_type=jnp.float32)

    def ladders(index, carry):
        both = jnp.concatenate([ladder_of(index), ladder_of(index + pairs // 2)], axis=1)
        shares[aux, pl.ds(pl.multiple_of(index * width, width), width), :] = both.astype(jnp.bfloat16)
        return carry

    lax.fori_loop(0, pairs // 2, ladders, 0)
    exchange = []
    for step in range(1, groups):
        copy = pltpu.make_async_remote_copy(
            src_ref=shares.at[aux],
            dst_ref=shares.at[aux],
            send_sem=aux_send.at[step - 1],
            recv_sem=aux_recv.at[step - 1],
            device_id={"aux": lax.rem(aux + step, groups)},
            device_id_type=MESH,
        )
        copy.start()
        exchange.append(copy)
    whole.wait_send()
    for way in range(2):
        @pl.when(can_send(way))
        def _(way=way):
            for side in range(2):
                first(way, side).wait_send()

        for far in range(1, last + 1):
            @pl.when(has_source(far, way))
            def _(far=far, way=way):
                for side in range(2):
                    handed(far, way, side).wait_send()
                    if far < last:
                        @pl.when(can_send(way))
                        def _(side=side):
                            link(far, way, side).wait_send()
    for step in range(1, groups):
        sender = lax.rem(aux + groups - step, groups)
        pltpu.make_async_remote_copy(
            src_ref=shares.at[aux], dst_ref=shares.at[sender],
            send_sem=aux_send.at[step - 1], recv_sem=aux_recv.at[step - 1],
            device_id={"aux": sender}, device_id_type=MESH,
        ).wait_recv()
        exchange[step - 1].wait_send()
    result = shares[0].astype(jnp.float32)
    for step in range(1, groups):
        result += shares[step].astype(jnp.float32)
    out_ref[...] = result


def fold_tiles(own_tile):
    count, rows, _ = own_tile.shape
    width = rows // 2
    row = lax.broadcasted_iota(jnp.int32, (width, rows), 0)
    lane = lax.broadcasted_iota(jnp.int32, (width, rows), 1)
    top, bottom = own_tile[:, :width], own_tile[:, width:]
    folded = jnp.where(lane >= row, top, jnp.roll(bottom, width, axis=2))
    folded = jnp.where(lane == row, folded * jnp.bfloat16(0.5), folded)
    edge = jnp.sum(jnp.where(lane == row + width, bottom.astype(jnp.float32) * 0.5, 0.0), axis=1)
    edge = edge.astype(jnp.bfloat16).reshape(count // 4, 4, rows)
    edge = jnp.pad(edge, ((0, 0), (0, 12), (0, 0))).reshape(2, -1, rows)
    return jnp.concatenate([folded.reshape(2, -1, rows), edge], axis=1)


def per_device_gathered(
    df_tiles, pno_coeffs, domains, amplitudes, exchange_ints, pno_energy, pair_shift, pno_count
):
    peers, groups = lax.axis_size("pair"), lax.axis_size("aux")
    pair_count, domain_blocks, pao_width, width = pno_coeffs.shape
    request_count = pair_count * domain_blocks
    depth = request_count // peers
    columns = jnp.arange(width, dtype=jnp.int32)
    live = columns[None, :] < pno_count[:, None]
    masked = jnp.where(live[:, None, None, :], pno_coeffs, jnp.zeros_like(pno_coeffs))
    targets = domains.reshape(request_count)
    order = jnp.arange(request_count, dtype=jnp.int32)
    earlier = (targets[:, None] == targets[None, :]) & (order[None, :] < order[:, None])
    slots = targets * depth + jnp.sum(earlier.astype(jnp.int32), axis=1)
    select = (slots[:, None] == order[None, :]).astype(jnp.bfloat16)
    coeffs = jnp.einsum(
        "rs,rnb->sbn", select, masked.reshape(request_count, pao_width, width),
        preferred_element_type=jnp.float32,
    ).astype(jnp.bfloat16)
    coeffs = coeffs.reshape(peers, depth * width, pao_width)
    both = live[:, :, None] & live[:, None, :]
    trial = jnp.where(both, amplitudes, jnp.zeros_like(amplitudes)).astype(jnp.bfloat16)
    twice = jnp.arange(2 * width, dtype=jnp.int32) // width
    trial = jnp.where(twice[:, None] == twice[None, :], jnp.tile(trial, (1, 2, 2)), jnp.bfloat16(0))
    packed = fold_tiles(df_tiles[0])
    rows = packed.shape[1]
    quarter = df_tiles.shape[1] // 2
    vmem = pl.BlockSpec(memory_space=pltpu.VMEM)
    dma = pltpu.SemaphoreType.DMA
    ladder = pl.pallas_call(
        functools.partial(ladder_kernel, depth=depth),
        out_shape=jax.ShapeDtypeStruct((pair_count // 2 * width, 2 * width), jnp.float32),
        in_specs=[vmem, vmem, pl.BlockSpec(memory_space=pltpu.SMEM), vmem],
        out_specs=vmem,
        scratch_shapes=[
            pltpu.VMEM((peers, 2, rows, pao_width), jnp.bfloat16),
            pltpu.VMEM((depth, quarter * width, pao_width), jnp.bfloat16),
            pltpu.VMEM((request_count, width, 2 * quarter * width), jnp.bfloat16),
            pltpu.VMEM((groups, pair_count // 2 * width, 2 * width), jnp.bfloat16),
            dma((4,)), dma((2 * peers,)), dma((2 * peers,)), dma((2 * peers,)), dma((2 * peers,)), dma((2,)),
            dma((groups - 1,)), dma((groups - 1,)),
        ],
        compiler_params=pltpu.CompilerParams(
            collective_id=0, has_side_effects=True, vmem_limit_bytes=48 * 1024 * 1024
        ),
        cost_estimate=pl.CostEstimate(flops=4000000000, bytes_accessed=4000000, transcendentals=0),
    )(packed, coeffs, slots, trial)
    ladder = ladder.reshape(pair_count // 2, width, 2, width).transpose(2, 0, 1, 3)
    ladder = ladder.reshape(pair_count, width, width)
    return apply_update(ladder, amplitudes, exchange_ints, pno_energy, pno_energy, pair_shift, both)


def solution(mesh):
    placed = (
        P("pair", "aux", None, None),
        P("pair", None, None, None),
        P("pair", None),
        P("pair", None, None),
        P("pair", None, None),
        P("pair", None),
        P("pair"),
        P("pair"),
    )
    body = per_device_gathered if mesh.shape["pair"] == 8 else per_device
    return jax.shard_map(
        body, mesh=mesh, in_specs=placed, out_specs=P("pair", None, None), check_vma=False
    )
```

```python
import functools
import math

import jax
import jax.numpy as jnp
from jax import lax
from jax.experimental import pallas as pl
from jax.experimental.pallas import tpu as pltpu
from jax.sharding import PartitionSpec as P


def apply_update(ladder, trial_amp, exch, energy_rows, energy_cols, shift, both):
    denom = energy_rows[:, :, None] + energy_cols[:, None, :] + shift[:, None, None]
    fresh = trial_amp - (exch + ladder) / denom
    return jnp.where(both, fresh, jnp.zeros_like(fresh))


def per_device(
    df_tiles, pno_coeffs, domains, amplitudes, exchange_ints, pno_energy, pair_shift, pno_count
):
    peers = lax.axis_size("pair")
    pair_count, domain_blocks, pao_width, pno_width = pno_coeffs.shape
    aux_local = df_tiles.shape[1]
    capacity = (pair_count * domain_blocks + peers - 1) // peers
    slot_count = peers * capacity
    request_count = pair_count * domain_blocks
    columns = jnp.arange(pno_width, dtype=jnp.int32)
    live = columns[None, :] < pno_count[:, None]
    masked = jnp.where(live[:, None, None, :], pno_coeffs, jnp.zeros_like(pno_coeffs))
    targets = domains.reshape(request_count)
    hits = (targets[:, None] == jnp.arange(peers, dtype=jnp.int32)[None, :]).astype(jnp.int32)
    before = jnp.cumsum(hits, axis=0) - hits
    ranks = jnp.sum(before * hits, axis=1)
    slots = targets * capacity + ranks
    select = (slots[:, None] == jnp.arange(slot_count, dtype=jnp.int32)[None, :]).astype(
        jnp.bfloat16
    )
    flat_coeffs = masked.reshape(request_count, pao_width * pno_width)
    outgoing = jnp.einsum(
        "rs,rk->sk", select, flat_coeffs, preferred_element_type=jnp.float32
    ).astype(jnp.bfloat16)
    outgoing = outgoing.reshape(peers, capacity, pao_width, pno_width)
    own_tile = df_tiles[0]
    arrived = lax.all_to_all(outgoing, "pair", split_axis=0, concat_axis=0, tiled=True)
    sources = arrived.shape[0]
    depth = arrived.shape[1]
    total = sources * depth
    group_size = math.gcd(total, 8)
    grouped = arrived.reshape(total // group_size, group_size, pao_width, pno_width)

    def project_group(group):
        half = jnp.einsum(
            "qmn,snp->sqmp", own_tile, group, preferred_element_type=jnp.float32
        ).astype(jnp.bfloat16)
        return jnp.einsum("smp,sqmr->sqpr", group, half, preferred_element_type=jnp.float32).astype(
            jnp.bfloat16
        )

    pieces = lax.map(project_group, grouped).reshape(
        sources, depth, aux_local, pno_width, pno_width
    )
    packed = pieces.reshape(sources, depth, aux_local * pno_width * pno_width)
    returned = lax.all_to_all(packed, "pair", split_axis=0, concat_axis=0, tiled=True)
    returned = returned.reshape(slot_count, returned.shape[2])
    owner_pair = jnp.arange(request_count, dtype=jnp.int32) // domain_blocks
    owner_sel = (owner_pair[:, None] == jnp.arange(pair_count, dtype=jnp.int32)[None, :]).astype(
        jnp.bfloat16
    )
    pair_sel = jnp.einsum(
        "rp,rs->ps", owner_sel, select, preferred_element_type=jnp.float32
    ).astype(jnp.bfloat16)
    sums = jnp.dot(pair_sel, returned, preferred_element_type=jnp.float32)
    full = sums.reshape(pair_count, aux_local, pno_width, pno_width)
    pair_ints = full.astype(jnp.bfloat16)
    both = live[:, :, None] & live[:, None, :]
    trial = jnp.where(both, amplitudes, jnp.zeros_like(amplitudes)).astype(jnp.bfloat16)
    inter = jnp.einsum(
        "pqac,pcd->pqad", pair_ints, trial, preferred_element_type=jnp.float32
    ).astype(jnp.bfloat16)
    partial_ladder = jnp.einsum(
        "pqad,pqbd->pab", inter, pair_ints, preferred_element_type=jnp.float32
    )
    ladder = lax.psum(partial_ladder.astype(jnp.bfloat16), "aux").astype(jnp.float32)
    return apply_update(ladder, amplitudes, exchange_ints, pno_energy, pno_energy, pair_shift, both)


MESH = pl.DeviceIdType.MESH


def ladder_kernel(packed_ref, coeff_ref, slot_ref, trial_ref, out_ref, tiles, halves, pieces,
                  shares, first_send, link_send, link_recv, pass_send, pass_recv, twin_sem, aux_send,
                  aux_recv,
                  *, depth):
    aux, pair = lax.axis_index("aux"), lax.axis_index("pair")
    peers, groups = tiles.shape[0], shares.shape[0]
    quarter = halves.shape[1] // (tiles.shape[3] // 2)
    width = tiles.shape[3] // 2
    pairs = trial_ref.shape[0]
    domain = slot_ref.shape[0] // pairs
    chip, core = pair // 2, pair % 2
    twin = chip * 2 + 1 - core
    last = peers // 2 - 1

    barrier = pltpu.get_barrier_semaphore()
    for step in range(1, peers):
        pl.semaphore_signal(barrier, inc=1, device_id={"pair": lax.rem(pair + step, peers)}, device_id_type=MESH)
    for step in range(1, groups):
        pl.semaphore_signal(barrier, inc=1, device_id={"aux": lax.rem(aux + step, groups)}, device_id_type=MESH)
    pl.semaphore_wait(barrier, peers + groups - 2)

    def remote(source, target, send, recv, where):
        return pltpu.make_async_remote_copy(
            src_ref=source, dst_ref=target, send_sem=send, recv_sem=recv,
            device_id={"pair": where}, device_id_type=MESH,
        )

    def onward(way):
        return chip + 1 if way == 0 else chip - 1

    def can_send(way):
        return chip < last if way == 0 else chip > 0

    def has_source(far, way):
        return chip >= far if way == 0 else chip + far <= last

    def block_of(far, way, side):
        return (chip - far if way == 0 else chip + far) * 2 + side

    def number(far, way, side):
        return ((far - 1) * 2 + way) * 2 + side

    def first(way, side):
        return remote(packed_ref.at[side], tiles.at[pair, side], first_send.at[way * 2 + side],
                      link_recv.at[number(1, way, core)], onward(way) * 2 + side)

    def link(far, way, side):
        block = block_of(far, way, side)
        return remote(tiles.at[block, core], tiles.at[block, core], link_send.at[number(far, way, side)],
                      link_recv.at[number(far + 1, way, side)], onward(way) * 2 + core)

    def incoming(far, way, side):
        block = block_of(far, way, side)
        return remote(packed_ref.at[0], tiles.at[block, core], link_send.at[number(far, way, side)],
                      link_recv.at[number(far, way, side)], twin)

    def handed(far, way, side):
        block = block_of(far, way, side)
        return remote(tiles.at[block, core], tiles.at[block, core], pass_send.at[number(far, way, side)],
                      pass_recv.at[number(far, way, side)], twin)

    def handed_here(far, way, side):
        block = block_of(far, way, side)
        return remote(packed_ref.at[0], tiles.at[block, 1 - core], pass_send.at[number(far, way, side)],
                      pass_recv.at[number(far, way, side)], twin)

    for way in range(2):
        @pl.when(can_send(way))
        def _(way=way):
            for side in range(2):
                first(way, side).start()

    whole = pltpu.make_async_remote_copy(
        src_ref=packed_ref,
        dst_ref=tiles.at[pair],
        send_sem=twin_sem.at[0],
        recv_sem=twin_sem.at[1],
        device_id={"pair": twin},
        device_id_type=MESH,
    )
    whole.start()

    row = lax.broadcasted_iota(jnp.int32, (width, 2 * width), 0)
    lane = lax.broadcasted_iota(jnp.int32, (width, 2 * width), 1)
    upper = lane >= row
    corner = lane == row + width
    unroll = 8

    def project(source, block, part):
        coeffs = coeff_ref[block]
        edges = source(pl.ds(quarter * width, quarter)).astype(jnp.float32)
        edge_row = lax.broadcasted_iota(jnp.int32, edges.shape, 0)

        def some(group, carry):
            for inner in range(unroll):
                aux_fn = group * unroll + inner
                first = pl.multiple_of(aux_fn * width, width)
                folded = source(pl.ds(first, width)).astype(jnp.float32)
                edge = jnp.sum(jnp.where(edge_row == aux_fn, edges, 0.0), axis=0, keepdims=True)
                top = jnp.where(upper, folded, 0.0)
                low = pltpu.roll(jnp.where(upper, 0.0, folded), width, 1)
                low = jnp.where(corner, edge, low)
                tri = jnp.concatenate([top, low], axis=0).astype(jnp.bfloat16)
                half = jnp.dot(coeffs, tri, preferred_element_type=jnp.float32)
                half += lax.dot_general(coeffs, tri, (((1,), (1,)), ((), ())), preferred_element_type=jnp.float32)
                half = half.astype(jnp.bfloat16)
                for rank in range(depth):
                    halves[rank, pl.ds(first, width), :] = half[rank * width:(rank + 1) * width]
            return carry

        lax.fori_loop(0, quarter // unroll, some, 0)
        span = quarter * width
        for rank in range(depth):
            piece = lax.dot_general(
                coeffs[rank * width:(rank + 1) * width], halves[rank],
                (((1,), (1,)), ((), ())), preferred_element_type=jnp.float32,
            )
            pieces[block * depth + rank, :, pl.ds(pl.multiple_of(part * span, span), span)] = piece.astype(jnp.bfloat16)

    def own(part, carry):
        project(lambda rows: packed_ref[part, rows, :], pair, part)
        return carry

    def arrived(block, part):
        project(lambda rows: tiles[block, part, rows, :], block, part)

    lax.fori_loop(0, 2, own, 0)
    whole.wait_recv()

    def from_twin(part, carry):
        arrived(twin, part)
        return carry

    lax.fori_loop(0, 2, from_twin, 0)

    for far in range(1, last):
        for way in range(2):
            @pl.when(has_source(far, way))
            def _(far=far, way=way):
                for side in range(2):
                    incoming(far, way, side).wait_recv()

                    @pl.when(can_send(way))
                    def _(side=side):
                        link(far, way, side).start()

                    handed(far, way, side).start()

        for way in range(2):
            @pl.when(has_source(far, way))
            def _(far=far, way=way):
                def direct(side, carry):
                    arrived(block_of(far, way, side), core)
                    return carry

                lax.fori_loop(0, 2, direct, 0)

        for way in range(2):
            @pl.when(has_source(far, way))
            def _(far=far, way=way):
                for side in range(2):
                    handed_here(far, way, side).wait_recv()

                def passed(side, carry):
                    arrived(block_of(far, way, side), 1 - core)
                    return carry

                lax.fori_loop(0, 2, passed, 0)

    for way in range(2):
        @pl.when(has_source(last, way))
        def _(way=way):
            for side in range(2):
                incoming(last, way, side).wait_recv()
                handed(last, way, side).start()
                arrived(block_of(last, way, side), core)
                handed_here(last, way, side).wait_recv()
                arrived(block_of(last, way, side), 1 - core)

    def ladder_of(index):
        total = pieces[slot_ref[index * domain]].astype(jnp.float32)
        for step in range(1, domain):
            total += pieces[slot_ref[index * domain + step]].astype(jnp.float32)
        ints = total.astype(jnp.bfloat16)
        trial = trial_ref[index]
        span = trial.shape[0]
        inter = jnp.concatenate(
            [
                jnp.dot(ints[:, at:at + span], trial, preferred_element_type=jnp.float32).astype(jnp.bfloat16)
                for at in range(0, ints.shape[1], span)
            ],
            axis=1,
        )
        return lax.dot_general(inter, ints, (((1,), (1,)), ((), ())), preferred_element_type=jnp.float32)

    def ladders(index, carry):
        both = jnp.concatenate([ladder_of(index), ladder_of(index + pairs // 2)], axis=1)
        shares[aux, pl.ds(pl.multiple_of(index * width, width), width), :] = both.astype(jnp.bfloat16)
        return carry

    lax.fori_loop(0, pairs // 2, ladders, 0)
    exchange = []
    for step in range(1, groups):
        copy = pltpu.make_async_remote_copy(
            src_ref=shares.at[aux],
            dst_ref=shares.at[aux],
            send_sem=aux_send.at[step - 1],
            recv_sem=aux_recv.at[step - 1],
            device_id={"aux": lax.rem(aux + step, groups)},
            device_id_type=MESH,
        )
        copy.start()
        exchange.append(copy)
    whole.wait_send()
    for way in range(2):
        @pl.when(can_send(way))
        def _(way=way):
            for side in range(2):
                first(way, side).wait_send()

        for far in range(1, last + 1):
            @pl.when(has_source(far, way))
            def _(far=far, way=way):
                for side in range(2):
                    handed(far, way, side).wait_send()
                    if far < last:
                        @pl.when(can_send(way))
                        def _(side=side):
                            link(far, way, side).wait_send()
    for step in range(1, groups):
        sender = lax.rem(aux + groups - step, groups)
        pltpu.make_async_remote_copy(
            src_ref=shares.at[aux], dst_ref=shares.at[sender],
            send_sem=aux_send.at[step - 1], recv_sem=aux_recv.at[step - 1],
            device_id={"aux": sender}, device_id_type=MESH,
        ).wait_recv()
        exchange[step - 1].wait_send()
    result = shares[0].astype(jnp.float32)
    for step in range(1, groups):
        result += shares[step].astype(jnp.float32)
    out_ref[...] = result


def fold_tiles(own_tile):
    count, rows, _ = own_tile.shape
    width = rows // 2
    row = lax.broadcasted_iota(jnp.int32, (width, rows), 0)
    lane = lax.broadcasted_iota(jnp.int32, (width, rows), 1)
    top, bottom = own_tile[:, :width], own_tile[:, width:]
    folded = jnp.where(lane >= row, top, jnp.roll(bottom, width, axis=2))
    folded = jnp.where(lane == row, folded * jnp.bfloat16(0.5), folded)
    edge = jnp.sum(jnp.where(lane == row + width, bottom.astype(jnp.float32) * 0.5, 0.0), axis=1)
    edge = edge.astype(jnp.bfloat16).reshape(2, count // 2, rows)
    return jnp.concatenate([folded.reshape(2, -1, rows), edge], axis=1)


def per_device_gathered(
    df_tiles, pno_coeffs, domains, amplitudes, exchange_ints, pno_energy, pair_shift, pno_count
):
    peers, groups = lax.axis_size("pair"), lax.axis_size("aux")
    pair_count, domain_blocks, pao_width, width = pno_coeffs.shape
    request_count = pair_count * domain_blocks
    depth = request_count // peers
    columns = jnp.arange(width, dtype=jnp.int32)
    live = columns[None, :] < pno_count[:, None]
    masked = jnp.where(live[:, None, None, :], pno_coeffs, jnp.zeros_like(pno_coeffs))
    targets = domains.reshape(request_count)
    order = jnp.arange(request_count, dtype=jnp.int32)
    earlier = (targets[:, None] == targets[None, :]) & (order[None, :] < order[:, None])
    slots = targets * depth + jnp.sum(earlier.astype(jnp.int32), axis=1)
    select = (slots[:, None] == order[None, :]).astype(jnp.bfloat16)
    coeffs = jnp.einsum(
        "rs,rnb->sbn", select, masked.reshape(request_count, pao_width, width),
        preferred_element_type=jnp.float32,
    ).astype(jnp.bfloat16)
    coeffs = coeffs.reshape(peers, depth * width, pao_width)
    both = live[:, :, None] & live[:, None, :]
    trial = jnp.where(both, amplitudes, jnp.zeros_like(amplitudes)).astype(jnp.bfloat16)
    twice = jnp.arange(2 * width, dtype=jnp.int32) // width
    trial = jnp.where(twice[:, None] == twice[None, :], jnp.tile(trial, (1, 2, 2)), jnp.bfloat16(0))
    packed = fold_tiles(df_tiles[0])
    rows = packed.shape[1]
    quarter = df_tiles.shape[1] // 2
    vmem = pl.BlockSpec(memory_space=pltpu.VMEM)
    dma = pltpu.SemaphoreType.DMA
    ladder = pl.pallas_call(
        functools.partial(ladder_kernel, depth=depth),
        out_shape=jax.ShapeDtypeStruct((pair_count // 2 * width, 2 * width), jnp.float32),
        in_specs=[vmem, vmem, pl.BlockSpec(memory_space=pltpu.SMEM), vmem],
        out_specs=vmem,
        scratch_shapes=[
            pltpu.VMEM((peers, 2, rows, pao_width), jnp.bfloat16),
            pltpu.VMEM((depth, quarter * width, pao_width), jnp.bfloat16),
            pltpu.VMEM((request_count, width, 2 * quarter * width), jnp.bfloat16),
            pltpu.VMEM((groups, pair_count // 2 * width, 2 * width), jnp.bfloat16),
            dma((4,)), dma((2 * peers,)), dma((2 * peers,)), dma((2 * peers,)), dma((2 * peers,)), dma((2,)),
            dma((groups - 1,)), dma((groups - 1,)),
        ],
        compiler_params=pltpu.CompilerParams(
            collective_id=0, has_side_effects=True, vmem_limit_bytes=48 * 1024 * 1024
        ),
        cost_estimate=pl.CostEstimate(flops=4000000000, bytes_accessed=4000000, transcendentals=0),
    )(packed, coeffs, slots, trial)
    ladder = ladder.reshape(pair_count // 2, width, 2, width).transpose(2, 0, 1, 3)
    ladder = ladder.reshape(pair_count, width, width)
    return apply_update(ladder, amplitudes, exchange_ints, pno_energy, pno_energy, pair_shift, both)


def solution(mesh):
    placed = (
        P("pair", "aux", None, None),
        P("pair", None, None, None),
        P("pair", None),
        P("pair", None, None),
        P("pair", None, None),
        P("pair", None),
        P("pair"),
        P("pair"),
    )
    body = per_device_gathered if mesh.shape["pair"] == 8 else per_device
    return jax.shard_map(
        body, mesh=mesh, in_specs=placed, out_specs=P("pair", None, None), check_vma=False
    )
```

```python
import functools
import math

import jax
import jax.numpy as jnp
from jax import lax
from jax.experimental import pallas as pl
from jax.experimental.pallas import tpu as pltpu
from jax.sharding import PartitionSpec as P


def apply_update(ladder, trial_amp, exch, energy_rows, energy_cols, shift, both):
    denom = energy_rows[:, :, None] + energy_cols[:, None, :] + shift[:, None, None]
    fresh = trial_amp - (exch + ladder) / denom
    return jnp.where(both, fresh, jnp.zeros_like(fresh))


def per_device(
    df_tiles, pno_coeffs, domains, amplitudes, exchange_ints, pno_energy, pair_shift, pno_count
):
    peers = lax.axis_size("pair")
    pair_count, domain_blocks, pao_width, pno_width = pno_coeffs.shape
    aux_local = df_tiles.shape[1]
    capacity = (pair_count * domain_blocks + peers - 1) // peers
    slot_count = peers * capacity
    request_count = pair_count * domain_blocks
    columns = jnp.arange(pno_width, dtype=jnp.int32)
    live = columns[None, :] < pno_count[:, None]
    masked = jnp.where(live[:, None, None, :], pno_coeffs, jnp.zeros_like(pno_coeffs))
    targets = domains.reshape(request_count)
    hits = (targets[:, None] == jnp.arange(peers, dtype=jnp.int32)[None, :]).astype(jnp.int32)
    before = jnp.cumsum(hits, axis=0) - hits
    ranks = jnp.sum(before * hits, axis=1)
    slots = targets * capacity + ranks
    select = (slots[:, None] == jnp.arange(slot_count, dtype=jnp.int32)[None, :]).astype(
        jnp.bfloat16
    )
    flat_coeffs = masked.reshape(request_count, pao_width * pno_width)
    outgoing = jnp.einsum(
        "rs,rk->sk", select, flat_coeffs, preferred_element_type=jnp.float32
    ).astype(jnp.bfloat16)
    outgoing = outgoing.reshape(peers, capacity, pao_width, pno_width)
    own_tile = df_tiles[0]
    arrived = lax.all_to_all(outgoing, "pair", split_axis=0, concat_axis=0, tiled=True)
    sources = arrived.shape[0]
    depth = arrived.shape[1]
    total = sources * depth
    group_size = math.gcd(total, 8)
    grouped = arrived.reshape(total // group_size, group_size, pao_width, pno_width)

    def project_group(group):
        half = jnp.einsum(
            "qmn,snp->sqmp", own_tile, group, preferred_element_type=jnp.float32
        ).astype(jnp.bfloat16)
        return jnp.einsum("smp,sqmr->sqpr", group, half, preferred_element_type=jnp.float32).astype(
            jnp.bfloat16
        )

    pieces = lax.map(project_group, grouped).reshape(
        sources, depth, aux_local, pno_width, pno_width
    )
    packed = pieces.reshape(sources, depth, aux_local * pno_width * pno_width)
    returned = lax.all_to_all(packed, "pair", split_axis=0, concat_axis=0, tiled=True)
    returned = returned.reshape(slot_count, returned.shape[2])
    owner_pair = jnp.arange(request_count, dtype=jnp.int32) // domain_blocks
    owner_sel = (owner_pair[:, None] == jnp.arange(pair_count, dtype=jnp.int32)[None, :]).astype(
        jnp.bfloat16
    )
    pair_sel = jnp.einsum(
        "rp,rs->ps", owner_sel, select, preferred_element_type=jnp.float32
    ).astype(jnp.bfloat16)
    sums = jnp.dot(pair_sel, returned, preferred_element_type=jnp.float32)
    full = sums.reshape(pair_count, aux_local, pno_width, pno_width)
    pair_ints = full.astype(jnp.bfloat16)
    both = live[:, :, None] & live[:, None, :]
    trial = jnp.where(both, amplitudes, jnp.zeros_like(amplitudes)).astype(jnp.bfloat16)
    inter = jnp.einsum(
        "pqac,pcd->pqad", pair_ints, trial, preferred_element_type=jnp.float32
    ).astype(jnp.bfloat16)
    partial_ladder = jnp.einsum(
        "pqad,pqbd->pab", inter, pair_ints, preferred_element_type=jnp.float32
    )
    ladder = lax.psum(partial_ladder.astype(jnp.bfloat16), "aux").astype(jnp.float32)
    return apply_update(ladder, amplitudes, exchange_ints, pno_energy, pno_energy, pair_shift, both)


MESH = pl.DeviceIdType.MESH


def ladder_kernel(tile_ref, coeff_ref, slot_ref, trial_ref, out_ref, packed_ref, tiles, halves,
                  pieces, shares, first_send, link_send, link_recv, pass_send, pass_recv, twin_sem, aux_send,
                  aux_recv,
                  *, depth):
    aux, pair = lax.axis_index("aux"), lax.axis_index("pair")
    peers, groups = tiles.shape[0], shares.shape[0]
    quarter = halves.shape[1] // (tiles.shape[3] // 2)
    width = tiles.shape[3] // 2
    pairs = trial_ref.shape[0]
    domain = slot_ref.shape[0] // pairs
    chip, core = pair // 2, pair % 2
    twin = chip * 2 + 1 - core
    last = peers // 2 - 1

    barrier = pltpu.get_barrier_semaphore()
    for step in range(1, peers):
        pl.semaphore_signal(barrier, inc=1, device_id={"pair": lax.rem(pair + step, peers)}, device_id_type=MESH)
    for step in range(1, groups):
        pl.semaphore_signal(barrier, inc=1, device_id={"aux": lax.rem(aux + step, groups)}, device_id_type=MESH)

    def remote(source, target, send, recv, where):
        return pltpu.make_async_remote_copy(
            src_ref=source, dst_ref=target, send_sem=send, recv_sem=recv,
            device_id={"pair": where}, device_id_type=MESH,
        )

    def onward(way):
        return chip + 1 if way == 0 else chip - 1

    def can_send(way):
        return chip < last if way == 0 else chip > 0

    def has_source(far, way):
        return chip >= far if way == 0 else chip + far <= last

    def block_of(far, way, side):
        return (chip - far if way == 0 else chip + far) * 2 + side

    def number(far, way, side):
        return ((far - 1) * 2 + way) * 2 + side

    def first(way, side):
        return remote(packed_ref.at[side], tiles.at[pair, side], first_send.at[way * 2 + side],
                      link_recv.at[number(1, way, core)], onward(way) * 2 + side)

    def link(far, way, side):
        block = block_of(far, way, side)
        return remote(tiles.at[block, core], tiles.at[block, core], link_send.at[number(far, way, side)],
                      link_recv.at[number(far + 1, way, side)], onward(way) * 2 + core)

    def incoming(far, way, side):
        block = block_of(far, way, side)
        return remote(packed_ref.at[0], tiles.at[block, core], link_send.at[number(far, way, side)],
                      link_recv.at[number(far, way, side)], twin)

    def handed(far, way, side):
        block = block_of(far, way, side)
        return remote(tiles.at[block, core], tiles.at[block, core], pass_send.at[number(far, way, side)],
                      pass_recv.at[number(far, way, side)], twin)

    def handed_here(far, way, side):
        block = block_of(far, way, side)
        return remote(packed_ref.at[0], tiles.at[block, 1 - core], pass_send.at[number(far, way, side)],
                      pass_recv.at[number(far, way, side)], twin)

    row = lax.broadcasted_iota(jnp.int32, (width, 2 * width), 0)
    lane = lax.broadcasted_iota(jnp.int32, (width, 2 * width), 1)
    upper = lane >= row
    corner = lane == row + width
    fold_row = lax.broadcasted_iota(jnp.int32, (quarter, 2 * width), 0)

    def fold(part):
        def some(group, edges):
            for inner in range(4):
                aux_fn = group * 4 + inner
                top = tile_ref[part * quarter + aux_fn, :width].astype(jnp.float32)
                bottom = tile_ref[part * quarter + aux_fn, width:].astype(jnp.float32)
                folded = jnp.where(upper, top, pltpu.roll(bottom, width, 1))
                folded = jnp.where(lane == row, folded * 0.5, folded)
                packed_ref[part, pl.ds(pl.multiple_of(aux_fn * width, width), width), :] = folded.astype(jnp.bfloat16)
                edge = jnp.sum(jnp.where(corner, bottom * 0.5, 0.0), axis=0, keepdims=True)
                edges = jnp.where(fold_row == aux_fn, edge, edges)
            return edges

        edges = lax.fori_loop(0, quarter // 4, some, jnp.zeros((quarter, 2 * width), jnp.float32))
        packed_ref[part, pl.ds(quarter * width, quarter), :] = edges.astype(jnp.bfloat16)

    for side in range(2):
        fold(side)
        if side == 0:
            pl.semaphore_wait(barrier, peers + groups - 2)
        for way in range(2):
            @pl.when(can_send(way))
            def _(way=way, side=side):
                first(way, side).start()

    whole = pltpu.make_async_remote_copy(
        src_ref=packed_ref,
        dst_ref=tiles.at[pair],
        send_sem=twin_sem.at[0],
        recv_sem=twin_sem.at[1],
        device_id={"pair": twin},
        device_id_type=MESH,
    )
    whole.start()

    unroll = 8

    def project(source, block, part):
        coeffs = coeff_ref[block]
        edges = source(pl.ds(quarter * width, quarter)).astype(jnp.float32)
        edge_row = lax.broadcasted_iota(jnp.int32, edges.shape, 0)

        def some(group, carry):
            for inner in range(unroll):
                aux_fn = group * unroll + inner
                first = pl.multiple_of(aux_fn * width, width)
                folded = source(pl.ds(first, width)).astype(jnp.float32)
                edge = jnp.sum(jnp.where(edge_row == aux_fn, edges, 0.0), axis=0, keepdims=True)
                top = jnp.where(upper, folded, 0.0)
                low = pltpu.roll(jnp.where(upper, 0.0, folded), width, 1)
                low = jnp.where(corner, edge, low)
                tri = jnp.concatenate([top, low], axis=0).astype(jnp.bfloat16)
                half = jnp.dot(coeffs, tri, preferred_element_type=jnp.float32)
                half += lax.dot_general(coeffs, tri, (((1,), (1,)), ((), ())), preferred_element_type=jnp.float32)
                half = half.astype(jnp.bfloat16)
                for rank in range(depth):
                    halves[rank, pl.ds(first, width), :] = half[rank * width:(rank + 1) * width]
            return carry

        lax.fori_loop(0, quarter // unroll, some, 0)
        span = quarter * width
        for rank in range(depth):
            piece = lax.dot_general(
                coeffs[rank * width:(rank + 1) * width], halves[rank],
                (((1,), (1,)), ((), ())), preferred_element_type=jnp.float32,
            )
            pieces[block * depth + rank, :, pl.ds(pl.multiple_of(part * span, span), span)] = piece.astype(jnp.bfloat16)

    def own(part, carry):
        project(lambda rows: packed_ref[part, rows, :], pair, part)
        return carry

    def arrived(block, part):
        project(lambda rows: tiles[block, part, rows, :], block, part)

    lax.fori_loop(0, 2, own, 0)
    whole.wait_recv()

    def from_twin(part, carry):
        arrived(twin, part)
        return carry

    lax.fori_loop(0, 2, from_twin, 0)

    for far in range(1, last):
        for way in range(2):
            @pl.when(has_source(far, way))
            def _(far=far, way=way):
                for side in range(2):
                    incoming(far, way, side).wait_recv()

                    @pl.when(can_send(way))
                    def _(side=side):
                        link(far, way, side).start()

                    handed(far, way, side).start()

        for way in range(2):
            @pl.when(has_source(far, way))
            def _(far=far, way=way):
                def direct(side, carry):
                    arrived(block_of(far, way, side), core)
                    return carry

                lax.fori_loop(0, 2, direct, 0)

        for way in range(2):
            @pl.when(has_source(far, way))
            def _(far=far, way=way):
                for side in range(2):
                    handed_here(far, way, side).wait_recv()

                def passed(side, carry):
                    arrived(block_of(far, way, side), 1 - core)
                    return carry

                lax.fori_loop(0, 2, passed, 0)

    for way in range(2):
        @pl.when(has_source(last, way))
        def _(way=way):
            for side in range(2):
                incoming(last, way, side).wait_recv()
                handed(last, way, side).start()
                arrived(block_of(last, way, side), core)
                handed_here(last, way, side).wait_recv()
                arrived(block_of(last, way, side), 1 - core)

    def ladder_of(index):
        total = pieces[slot_ref[index * domain]].astype(jnp.float32)
        for step in range(1, domain):
            total += pieces[slot_ref[index * domain + step]].astype(jnp.float32)
        ints = total.astype(jnp.bfloat16)
        trial = trial_ref[index]
        span = trial.shape[0]
        inter = jnp.concatenate(
            [
                jnp.dot(ints[:, at:at + span], trial, preferred_element_type=jnp.float32).astype(jnp.bfloat16)
                for at in range(0, ints.shape[1], span)
            ],
            axis=1,
        )
        return lax.dot_general(inter, ints, (((1,), (1,)), ((), ())), preferred_element_type=jnp.float32)

    def ladders(index, carry):
        both = jnp.concatenate([ladder_of(index), ladder_of(index + pairs // 2)], axis=1)
        shares[aux, pl.ds(pl.multiple_of(index * width, width), width), :] = both.astype(jnp.bfloat16)
        return carry

    lax.fori_loop(0, pairs // 2, ladders, 0, unroll=True)
    exchange = []
    for step in range(1, groups):
        copy = pltpu.make_async_remote_copy(
            src_ref=shares.at[aux],
            dst_ref=shares.at[aux],
            send_sem=aux_send.at[step - 1],
            recv_sem=aux_recv.at[step - 1],
            device_id={"aux": lax.rem(aux + step, groups)},
            device_id_type=MESH,
        )
        copy.start()
        exchange.append(copy)
    whole.wait_send()
    for way in range(2):
        @pl.when(can_send(way))
        def _(way=way):
            for side in range(2):
                first(way, side).wait_send()

        for far in range(1, last + 1):
            @pl.when(has_source(far, way))
            def _(far=far, way=way):
                for side in range(2):
                    handed(far, way, side).wait_send()
                    if far < last:
                        @pl.when(can_send(way))
                        def _(side=side):
                            link(far, way, side).wait_send()
    for step in range(1, groups):
        sender = lax.rem(aux + groups - step, groups)
        pltpu.make_async_remote_copy(
            src_ref=shares.at[aux], dst_ref=shares.at[sender],
            send_sem=aux_send.at[step - 1], recv_sem=aux_recv.at[step - 1],
            device_id={"aux": sender}, device_id_type=MESH,
        ).wait_recv()
        exchange[step - 1].wait_send()
    result = shares[0].astype(jnp.float32)
    for step in range(1, groups):
        result += shares[step].astype(jnp.float32)
    out_ref[...] = result


def per_device_gathered(
    df_tiles, pno_coeffs, domains, amplitudes, exchange_ints, pno_energy, pair_shift, pno_count
):
    peers, groups = lax.axis_size("pair"), lax.axis_size("aux")
    pair_count, domain_blocks, pao_width, width = pno_coeffs.shape
    request_count = pair_count * domain_blocks
    depth = request_count // peers
    columns = jnp.arange(width, dtype=jnp.int32)
    live = columns[None, :] < pno_count[:, None]
    masked = jnp.where(live[:, None, None, :], pno_coeffs, jnp.zeros_like(pno_coeffs))
    targets = domains.reshape(request_count)
    order = jnp.arange(request_count, dtype=jnp.int32)
    earlier = (targets[:, None] == targets[None, :]) & (order[None, :] < order[:, None])
    slots = targets * depth + jnp.sum(earlier.astype(jnp.int32), axis=1)
    select = (slots[:, None] == order[None, :]).astype(jnp.bfloat16)
    coeffs = jnp.einsum(
        "rs,rnb->sbn", select, masked.reshape(request_count, pao_width, width),
        preferred_element_type=jnp.float32,
    ).astype(jnp.bfloat16)
    coeffs = coeffs.reshape(peers, depth * width, pao_width)
    both = live[:, :, None] & live[:, None, :]
    trial = jnp.where(both, amplitudes, jnp.zeros_like(amplitudes)).astype(jnp.bfloat16)
    before, after = (0, width), (width, 0)
    trial = jnp.pad(trial, ((0, 0), before, before)) + jnp.pad(trial, ((0, 0), after, after))
    quarter = df_tiles.shape[1] // 2
    rows = quarter * (width + 1)
    vmem = pl.BlockSpec(memory_space=pltpu.VMEM)
    dma = pltpu.SemaphoreType.DMA
    ladder = pl.pallas_call(
        functools.partial(ladder_kernel, depth=depth),
        out_shape=jax.ShapeDtypeStruct((pair_count // 2 * width, 2 * width), jnp.float32),
        in_specs=[vmem, vmem, pl.BlockSpec(memory_space=pltpu.SMEM), vmem],
        out_specs=vmem,
        scratch_shapes=[
            pltpu.VMEM((2, rows, pao_width), jnp.bfloat16),
            pltpu.VMEM((peers, 2, rows, pao_width), jnp.bfloat16),
            pltpu.VMEM((depth, quarter * width, pao_width), jnp.bfloat16),
            pltpu.VMEM((request_count, width, 2 * quarter * width), jnp.bfloat16),
            pltpu.VMEM((groups, pair_count // 2 * width, 2 * width), jnp.bfloat16),
            dma((4,)), dma((2 * peers,)), dma((2 * peers,)), dma((2 * peers,)), dma((2 * peers,)), dma((2,)),
            dma((groups - 1,)), dma((groups - 1,)),
        ],
        compiler_params=pltpu.CompilerParams(
            collective_id=0, has_side_effects=True, vmem_limit_bytes=48 * 1024 * 1024
        ),
        cost_estimate=pl.CostEstimate(flops=4000000000, bytes_accessed=4000000, transcendentals=0),
    )(df_tiles[0], coeffs, slots, trial)
    ladder = ladder.reshape(pair_count // 2, width, 2, width).transpose(2, 0, 1, 3)
    ladder = ladder.reshape(pair_count, width, width)
    return apply_update(ladder, amplitudes, exchange_ints, pno_energy, pno_energy, pair_shift, both)


def solution(mesh):
    placed = (
        P("pair", "aux", None, None),
        P("pair", None, None, None),
        P("pair", None),
        P("pair", None, None),
        P("pair", None, None),
        P("pair", None),
        P("pair"),
        P("pair"),
    )
    body = per_device_gathered if mesh.shape["pair"] == 8 else per_device
    return jax.shard_map(
        body, mesh=mesh, in_specs=placed, out_specs=P("pair", None, None), check_vma=False
    )
```

```python
import functools
import math

import jax
import jax.numpy as jnp
from jax import lax
from jax.experimental import pallas as pl
from jax.experimental.pallas import tpu as pltpu
from jax.sharding import PartitionSpec as P


def apply_update(ladder, trial_amp, exch, energy_rows, energy_cols, shift, both):
    denom = energy_rows[:, :, None] + energy_cols[:, None, :] + shift[:, None, None]
    fresh = trial_amp - (exch + ladder) / denom
    return jnp.where(both, fresh, jnp.zeros_like(fresh))


def per_device(
    df_tiles, pno_coeffs, domains, amplitudes, exchange_ints, pno_energy, pair_shift, pno_count
):
    peers = lax.axis_size("pair")
    pair_count, domain_blocks, pao_width, pno_width = pno_coeffs.shape
    aux_local = df_tiles.shape[1]
    capacity = (pair_count * domain_blocks + peers - 1) // peers
    slot_count = peers * capacity
    request_count = pair_count * domain_blocks
    columns = jnp.arange(pno_width, dtype=jnp.int32)
    live = columns[None, :] < pno_count[:, None]
    masked = jnp.where(live[:, None, None, :], pno_coeffs, jnp.zeros_like(pno_coeffs))
    targets = domains.reshape(request_count)
    hits = (targets[:, None] == jnp.arange(peers, dtype=jnp.int32)[None, :]).astype(jnp.int32)
    before = jnp.cumsum(hits, axis=0) - hits
    ranks = jnp.sum(before * hits, axis=1)
    slots = targets * capacity + ranks
    select = (slots[:, None] == jnp.arange(slot_count, dtype=jnp.int32)[None, :]).astype(
        jnp.bfloat16
    )
    flat_coeffs = masked.reshape(request_count, pao_width * pno_width)
    outgoing = jnp.einsum(
        "rs,rk->sk", select, flat_coeffs, preferred_element_type=jnp.float32
    ).astype(jnp.bfloat16)
    outgoing = outgoing.reshape(peers, capacity, pao_width, pno_width)
    own_tile = df_tiles[0]
    arrived = lax.all_to_all(outgoing, "pair", split_axis=0, concat_axis=0, tiled=True)
    sources = arrived.shape[0]
    depth = arrived.shape[1]
    total = sources * depth
    group_size = math.gcd(total, 8)
    grouped = arrived.reshape(total // group_size, group_size, pao_width, pno_width)

    def project_group(group):
        half = jnp.einsum(
            "qmn,snp->sqmp", own_tile, group, preferred_element_type=jnp.float32
        ).astype(jnp.bfloat16)
        return jnp.einsum("smp,sqmr->sqpr", group, half, preferred_element_type=jnp.float32).astype(
            jnp.bfloat16
        )

    pieces = lax.map(project_group, grouped).reshape(
        sources, depth, aux_local, pno_width, pno_width
    )
    packed = pieces.reshape(sources, depth, aux_local * pno_width * pno_width)
    returned = lax.all_to_all(packed, "pair", split_axis=0, concat_axis=0, tiled=True)
    returned = returned.reshape(slot_count, returned.shape[2])
    owner_pair = jnp.arange(request_count, dtype=jnp.int32) // domain_blocks
    owner_sel = (owner_pair[:, None] == jnp.arange(pair_count, dtype=jnp.int32)[None, :]).astype(
        jnp.bfloat16
    )
    pair_sel = jnp.einsum(
        "rp,rs->ps", owner_sel, select, preferred_element_type=jnp.float32
    ).astype(jnp.bfloat16)
    sums = jnp.dot(pair_sel, returned, preferred_element_type=jnp.float32)
    full = sums.reshape(pair_count, aux_local, pno_width, pno_width)
    pair_ints = full.astype(jnp.bfloat16)
    both = live[:, :, None] & live[:, None, :]
    trial = jnp.where(both, amplitudes, jnp.zeros_like(amplitudes)).astype(jnp.bfloat16)
    inter = jnp.einsum(
        "pqac,pcd->pqad", pair_ints, trial, preferred_element_type=jnp.float32
    ).astype(jnp.bfloat16)
    partial_ladder = jnp.einsum(
        "pqad,pqbd->pab", inter, pair_ints, preferred_element_type=jnp.float32
    )
    ladder = lax.psum(partial_ladder.astype(jnp.bfloat16), "aux").astype(jnp.float32)
    return apply_update(ladder, amplitudes, exchange_ints, pno_energy, pno_energy, pair_shift, both)


MESH = pl.DeviceIdType.MESH


def ladder_kernel(tile_ref, coeff_ref, slot_ref, trial_ref, out_ref, packed_ref, tiles, halves,
                  pieces, shares, first_send, link_send, link_recv, pass_send, pass_recv, twin_sem, aux_send,
                  aux_recv,
                  *, depth):
    aux, pair = lax.axis_index("aux"), lax.axis_index("pair")
    peers, groups = tiles.shape[0], shares.shape[0]
    quarter = halves.shape[1] // (tiles.shape[3] // 2)
    width = tiles.shape[3] // 2
    pairs = trial_ref.shape[0]
    domain = slot_ref.shape[0] // pairs
    chip, core = pair // 2, pair % 2
    twin = chip * 2 + 1 - core
    last = peers // 2 - 1

    barrier = pltpu.get_barrier_semaphore()
    for step in range(1, peers):
        pl.semaphore_signal(barrier, inc=1, device_id={"pair": lax.rem(pair + step, peers)}, device_id_type=MESH)
    for step in range(1, groups):
        pl.semaphore_signal(barrier, inc=1, device_id={"aux": lax.rem(aux + step, groups)}, device_id_type=MESH)

    def remote(source, target, send, recv, where):
        return pltpu.make_async_remote_copy(
            src_ref=source, dst_ref=target, send_sem=send, recv_sem=recv,
            device_id={"pair": where}, device_id_type=MESH,
        )

    def onward(way):
        return chip + 1 if way == 0 else chip - 1

    def can_send(way):
        return chip < last if way == 0 else chip > 0

    def has_source(far, way):
        return chip >= far if way == 0 else chip + far <= last

    def block_of(far, way, side):
        return (chip - far if way == 0 else chip + far) * 2 + side

    def number(far, way, side):
        return ((far - 1) * 2 + way) * 2 + side

    def first(way, side):
        return remote(packed_ref.at[side], tiles.at[pair, side], first_send.at[way * 2 + side],
                      link_recv.at[number(1, way, core)], onward(way) * 2 + side)

    def link(far, way, side):
        block = block_of(far, way, side)
        return remote(tiles.at[block, core], tiles.at[block, core], link_send.at[number(far, way, side)],
                      link_recv.at[number(far + 1, way, side)], onward(way) * 2 + core)

    def incoming(far, way, side):
        block = block_of(far, way, side)
        return remote(packed_ref.at[0], tiles.at[block, core], link_send.at[number(far, way, side)],
                      link_recv.at[number(far, way, side)], twin)

    def handed(far, way, side):
        block = block_of(far, way, side)
        return remote(tiles.at[block, core], tiles.at[block, core], pass_send.at[number(far, way, side)],
                      pass_recv.at[number(far, way, side)], twin)

    def handed_here(far, way, side):
        block = block_of(far, way, side)
        return remote(packed_ref.at[0], tiles.at[block, 1 - core], pass_send.at[number(far, way, side)],
                      pass_recv.at[number(far, way, side)], twin)

    row = lax.broadcasted_iota(jnp.int32, (width, 2 * width), 0)
    lane = lax.broadcasted_iota(jnp.int32, (width, 2 * width), 1)
    upper = lane >= row
    corner = lane == row + width
    fold_row = lax.broadcasted_iota(jnp.int32, (quarter, 2 * width), 0)

    def fold(part):
        def some(group, edges):
            for inner in range(4):
                aux_fn = group * 4 + inner
                top = tile_ref[part * quarter + aux_fn, :width].astype(jnp.float32)
                bottom = tile_ref[part * quarter + aux_fn, width:].astype(jnp.float32)
                folded = jnp.where(upper, top, pltpu.roll(bottom, width, 1))
                folded = jnp.where(lane == row, folded * 0.5, folded)
                packed_ref[part, pl.ds(pl.multiple_of(aux_fn * width, width), width), :] = folded.astype(jnp.bfloat16)
                edge = jnp.sum(jnp.where(corner, bottom * 0.5, 0.0), axis=0, keepdims=True)
                edges = jnp.where(fold_row == aux_fn, edge, edges)
            return edges

        edges = lax.fori_loop(0, quarter // 4, some, jnp.zeros((quarter, 2 * width), jnp.float32))
        packed_ref[part, pl.ds(quarter * width, quarter), :] = edges.astype(jnp.bfloat16)

    for side in range(2):
        fold(side)
        if side == 0:
            pl.semaphore_wait(barrier, peers + groups - 2)
        for way in range(2):
            @pl.when(can_send(way))
            def _(way=way, side=side):
                first(way, side).start()

    whole = pltpu.make_async_remote_copy(
        src_ref=packed_ref,
        dst_ref=tiles.at[pair],
        send_sem=twin_sem.at[0],
        recv_sem=twin_sem.at[1],
        device_id={"pair": twin},
        device_id_type=MESH,
    )
    whole.start()

    unroll = 16

    def project(source, block, part):
        coeffs = coeff_ref[block]
        edges = source(pl.ds(quarter * width, quarter)).astype(jnp.float32)
        edge_row = lax.broadcasted_iota(jnp.int32, edges.shape, 0)

        def some(group, carry):
            for inner in range(unroll):
                aux_fn = group * unroll + inner
                first = pl.multiple_of(aux_fn * width, width)
                folded = source(pl.ds(first, width)).astype(jnp.float32)
                edge = jnp.sum(jnp.where(edge_row == aux_fn, edges, 0.0), axis=0, keepdims=True)
                top = jnp.where(upper, folded, 0.0)
                low = pltpu.roll(jnp.where(upper, 0.0, folded), width, 1)
                low = jnp.where(corner, edge, low)
                tri = jnp.concatenate([top, low], axis=0).astype(jnp.bfloat16)
                half = jnp.dot(coeffs, tri, preferred_element_type=jnp.float32)
                half += lax.dot_general(coeffs, tri, (((1,), (1,)), ((), ())), preferred_element_type=jnp.float32)
                half = half.astype(jnp.bfloat16)
                for rank in range(depth):
                    halves[rank, pl.ds(first, width), :] = half[rank * width:(rank + 1) * width]
            return carry

        lax.fori_loop(0, quarter // unroll, some, 0)
        span = quarter * width
        for rank in range(depth):
            piece = lax.dot_general(
                coeffs[rank * width:(rank + 1) * width], halves[rank],
                (((1,), (1,)), ((), ())), preferred_element_type=jnp.float32,
            )
            pieces[block * depth + rank, :, pl.ds(pl.multiple_of(part * span, span), span)] = piece.astype(jnp.bfloat16)

    def own(part, carry):
        project(lambda rows: packed_ref[part, rows, :], pair, part)
        return carry

    def arrived(block, part):
        project(lambda rows: tiles[block, part, rows, :], block, part)

    lax.fori_loop(0, 2, own, 0)
    whole.wait_recv()

    def from_twin(part, carry):
        arrived(twin, part)
        return carry

    lax.fori_loop(0, 2, from_twin, 0)

    for far in range(1, last):
        for way in range(2):
            @pl.when(has_source(far, way))
            def _(far=far, way=way):
                for side in range(2):
                    incoming(far, way, side).wait_recv()

                    @pl.when(can_send(way))
                    def _(side=side):
                        link(far, way, side).start()

                    handed(far, way, side).start()

        for way in range(2):
            @pl.when(has_source(far, way))
            def _(far=far, way=way):
                def direct(side, carry):
                    arrived(block_of(far, way, side), core)
                    return carry

                lax.fori_loop(0, 2, direct, 0)

        for way in range(2):
            @pl.when(has_source(far, way))
            def _(far=far, way=way):
                for side in range(2):
                    handed_here(far, way, side).wait_recv()

                def passed(side, carry):
                    arrived(block_of(far, way, side), 1 - core)
                    return carry

                lax.fori_loop(0, 2, passed, 0)

    for way in range(2):
        @pl.when(has_source(last, way))
        def _(way=way):
            for side in range(2):
                incoming(last, way, side).wait_recv()
                handed(last, way, side).start()
                arrived(block_of(last, way, side), core)
                handed_here(last, way, side).wait_recv()
                arrived(block_of(last, way, side), 1 - core)

    def ladder_of(index):
        total = pieces[slot_ref[index * domain]].astype(jnp.float32)
        for step in range(1, domain):
            total += pieces[slot_ref[index * domain + step]].astype(jnp.float32)
        ints = total.astype(jnp.bfloat16)
        trial = trial_ref[index]
        span = trial.shape[0]
        inter = jnp.concatenate(
            [
                jnp.dot(ints[:, at:at + span], trial, preferred_element_type=jnp.float32).astype(jnp.bfloat16)
                for at in range(0, ints.shape[1], span)
            ],
            axis=1,
        )
        return lax.dot_general(inter, ints, (((1,), (1,)), ((), ())), preferred_element_type=jnp.float32)

    def ladders(index, carry):
        both = jnp.concatenate([ladder_of(index), ladder_of(index + pairs // 2)], axis=1)
        shares[aux, pl.ds(pl.multiple_of(index * width, width), width), :] = both.astype(jnp.bfloat16)
        return carry

    lax.fori_loop(0, pairs // 2, ladders, 0, unroll=True)
    exchange = []
    for step in range(1, groups):
        copy = pltpu.make_async_remote_copy(
            src_ref=shares.at[aux],
            dst_ref=shares.at[aux],
            send_sem=aux_send.at[step - 1],
            recv_sem=aux_recv.at[step - 1],
            device_id={"aux": lax.rem(aux + step, groups)},
            device_id_type=MESH,
        )
        copy.start()
        exchange.append(copy)
    whole.wait_send()
    for way in range(2):
        @pl.when(can_send(way))
        def _(way=way):
            for side in range(2):
                first(way, side).wait_send()

        for far in range(1, last + 1):
            @pl.when(has_source(far, way))
            def _(far=far, way=way):
                for side in range(2):
                    handed(far, way, side).wait_send()
                    if far < last:
                        @pl.when(can_send(way))
                        def _(side=side):
                            link(far, way, side).wait_send()
    for step in range(1, groups):
        sender = lax.rem(aux + groups - step, groups)
        pltpu.make_async_remote_copy(
            src_ref=shares.at[aux], dst_ref=shares.at[sender],
            send_sem=aux_send.at[step - 1], recv_sem=aux_recv.at[step - 1],
            device_id={"aux": sender}, device_id_type=MESH,
        ).wait_recv()
        exchange[step - 1].wait_send()
    result = shares[0].astype(jnp.float32)
    for step in range(1, groups):
        result += shares[step].astype(jnp.float32)
    out_ref[...] = result


def per_device_gathered(
    df_tiles, pno_coeffs, domains, amplitudes, exchange_ints, pno_energy, pair_shift, pno_count
):
    peers, groups = lax.axis_size("pair"), lax.axis_size("aux")
    pair_count, domain_blocks, pao_width, width = pno_coeffs.shape
    request_count = pair_count * domain_blocks
    depth = request_count // peers
    columns = jnp.arange(width, dtype=jnp.int32)
    live = columns[None, :] < pno_count[:, None]
    masked = jnp.where(live[:, None, None, :], pno_coeffs, jnp.zeros_like(pno_coeffs))
    targets = domains.reshape(request_count)
    order = jnp.arange(request_count, dtype=jnp.int32)
    earlier = (targets[:, None] == targets[None, :]) & (order[None, :] < order[:, None])
    slots = targets * depth + jnp.sum(earlier.astype(jnp.int32), axis=1)
    select = (slots[:, None] == order[None, :]).astype(jnp.bfloat16)
    coeffs = jnp.einsum(
        "rs,rnb->sbn", select, masked.reshape(request_count, pao_width, width),
        preferred_element_type=jnp.float32,
    ).astype(jnp.bfloat16)
    coeffs = coeffs.reshape(peers, depth * width, pao_width)
    both = live[:, :, None] & live[:, None, :]
    trial = jnp.where(both, amplitudes, jnp.zeros_like(amplitudes)).astype(jnp.bfloat16)
    before, after = (0, width), (width, 0)
    trial = jnp.pad(trial, ((0, 0), before, before)) + jnp.pad(trial, ((0, 0), after, after))
    quarter = df_tiles.shape[1] // 2
    rows = quarter * (width + 1)
    vmem = pl.BlockSpec(memory_space=pltpu.VMEM)
    dma = pltpu.SemaphoreType.DMA
    ladder = pl.pallas_call(
        functools.partial(ladder_kernel, depth=depth),
        out_shape=jax.ShapeDtypeStruct((pair_count // 2 * width, 2 * width), jnp.float32),
        in_specs=[vmem, vmem, pl.BlockSpec(memory_space=pltpu.SMEM), vmem],
        out_specs=vmem,
        scratch_shapes=[
            pltpu.VMEM((2, rows, pao_width), jnp.bfloat16),
            pltpu.VMEM((peers, 2, rows, pao_width), jnp.bfloat16),
            pltpu.VMEM((depth, quarter * width, pao_width), jnp.bfloat16),
            pltpu.VMEM((request_count, width, 2 * quarter * width), jnp.bfloat16),
            pltpu.VMEM((groups, pair_count // 2 * width, 2 * width), jnp.bfloat16),
            dma((4,)), dma((2 * peers,)), dma((2 * peers,)), dma((2 * peers,)), dma((2 * peers,)), dma((2,)),
            dma((groups - 1,)), dma((groups - 1,)),
        ],
        compiler_params=pltpu.CompilerParams(
            collective_id=0, has_side_effects=True, vmem_limit_bytes=48 * 1024 * 1024
        ),
        cost_estimate=pl.CostEstimate(flops=4000000000, bytes_accessed=4000000, transcendentals=0),
    )(df_tiles[0], coeffs, slots, trial)
    ladder = ladder.reshape(pair_count // 2, width, 2, width).transpose(2, 0, 1, 3)
    ladder = ladder.reshape(pair_count, width, width)
    return apply_update(ladder, amplitudes, exchange_ints, pno_energy, pno_energy, pair_shift, both)


def solution(mesh):
    placed = (
        P("pair", "aux", None, None),
        P("pair", None, None, None),
        P("pair", None),
        P("pair", None, None),
        P("pair", None, None),
        P("pair", None),
        P("pair"),
        P("pair"),
    )
    body = per_device_gathered if mesh.shape["pair"] == 8 else per_device
    return jax.shard_map(
        body, mesh=mesh, in_specs=placed, out_specs=P("pair", None, None), check_vma=False
    )
```
